32 devices in a mesh: lon: 8 (over z, y), lat: 2 (over x), tp: 2 (over core).
Axes of the slice: x: 2, y: 2, z: 4, core: 2. Of those that a mesh axis runs over, the one named last changes fastest.
Arguments:
- tokens: bfloat16 [2, 32, 256, 1024], P('tp', 'lat', 'lon'), may hold values from -6 to 6
- qkv_weight: bfloat16 [3, 1024, 1024], P(None, None, 'tp'), may hold values from -0.1875 to 0.1875
- proj_weight: bfloat16 [1024, 1024], P('tp'), may hold values from -0.1875 to 0.1875
- up_weight: bfloat16 [1024, 4096], P(None, 'tp'), may hold values from -0.1875 to 0.1875
- down_weight: bfloat16 [4096, 1024], P('tp'), may hold values from -0.09375 to 0.09375
- pos_bias: bfloat16 [16, 128, 128], P('tp'), may hold values from -400 to 400
- class_bias: bfloat16 [8, 16, 128], P(None, 'tp'), may hold values from -4 to 4
- surface_class: int32 [32, 256], P('lat', 'lon'), may hold values from 0 to 7
Outputs:
- layer_out: bfloat16 [2, 32, 256, 1024], P('tp', 'lat', 'lon')
The draws below stay inside these ranges and needn't reach their ends.
All inputs are finite; a program needn't handle non-finite values.
Results may differ from the reference program's by a relative error of at most 0.01.
Values may be sent and summed in bfloat16 or wider, within the bound.
A program may use at most 128 MiB of HBM per device.

```python
import jax
import jax.numpy as jnp
from jax import lax

D = 1024
HEADS = 16
HEAD_DIM = 64
FF = 4096
LEV = 2
CLASSES = 8
WT = 128
NLAT = 32
NLON = 256


def draw_pos_bias(key, part):
    key = jax.random.fold_in(key, 11)
    base = jax.random.normal(key, (HEADS, WT, WT), jnp.float32)
    return base.astype(jnp.bfloat16)


def touch_ends(drawn, rng, least, largest):
    place = [jax.random.randint(jax.random.fold_in(rng, axis), (), 0, length) for axis, length in enumerate(drawn.shape)]
    main_axis = drawn.shape.index(max(drawn.shape))
    next_to = place[:main_axis] + [(place[main_axis] + 1) % drawn.shape[main_axis]] + place[main_axis + 1:]
    return drawn.at[tuple(place)].set(least).at[tuple(next_to)].set(largest)


def block_levels(rng, shape, cuts, smallest, high):
    factor_of, own = 1.0, jax.random.fold_in(rng, 6)
    for axis_at, parts in cuts:
        steps = jnp.exp(jax.random.uniform(jax.random.fold_in(own, axis_at), (parts,), jnp.float32, smallest / len(cuts), high / len(cuts)))
        factor_of = factor_of * jnp.repeat(steps, shape[axis_at] // parts).reshape([-1 if axis == axis_at else 1 for axis in range(len(shape))])
    return factor_of


def noise(stream_key, dims, width, reach, pieces=(), kind=jnp.bfloat16):
    entries = jax.random.normal(stream_key, dims, jnp.float32) * width
    if len(pieces) > 0:
        entries = block_levels(stream_key, dims, pieces, -0.22, 0.18) * entries
    return jnp.clip(entries, min=-reach, max=reach).astype(kind)


def setup_inputs(seed: int = 0) -> dict:
    streams_of = jax.random.split(jax.random.key(seed), 9)
    tokens = noise(streams_of[0], (LEV, NLAT, NLON, D), 1.0, 6.0, ((0, 2), (1, 2), (2, 8)))
    qkv_weight = noise(streams_of[1], (3, D, D), D ** -0.5, 0.1875, ((2, 2),))
    proj_weight = noise(streams_of[2], (D, D), D ** -0.5, 0.1875, ((0, 2),))
    up_weight = noise(streams_of[3], (D, FF), D ** -0.5, 0.1875, ((1, 2),))
    down_weight = noise(streams_of[4], (FF, D), FF ** -0.5, 0.09375, ((0, 2),))
    pos_bias = draw_pos_bias(jax.random.fold_in(streams_of[8], 71), 0)
    class_bias = noise(streams_of[6], (CLASSES, HEADS, WT), 1.0, 4.0, ((1, 2),))
    surface_class = touch_ends(jax.random.randint(streams_of[7], (NLAT, NLON), 0, CLASSES), jax.random.fold_in(streams_of[7], 1), 0, CLASSES - 1).astype(jnp.int32)
    return dict(tokens=tokens, qkv_weight=qkv_weight, proj_weight=proj_weight, up_weight=up_weight, down_weight=down_weight, pos_bias=pos_bias, class_bias=class_bias, surface_class=surface_class)


def layer_norm(values):
    mean_value = lax.optimization_barrier(jnp.mean(values, axis=-1, keepdims=True))
    centred = values - mean_value
    variance = lax.optimization_barrier(jnp.mean(centred * centred, axis=-1, keepdims=True))
    return centred * lax.rsqrt(variance + 1e-05)

def attend(query, keys, values, bias, allowed):
    count = query.shape[0]
    q_four = query.astype(jnp.float32).reshape(count, WT, HEADS, HEAD_DIM)
    k_four = keys.astype(jnp.float32).reshape(count, WT, HEADS, HEAD_DIM)
    v_four = values.astype(jnp.float32).reshape(count, WT, HEADS, HEAD_DIM)
    scores = jnp.einsum('wihc,wjhc->whij', q_four, k_four) * HEAD_DIM ** (-0.5) + bias
    scores = jnp.where(allowed[:, None, None, :], scores, -jnp.inf)
    top = lax.optimization_barrier(jnp.max(scores, axis=-1, keepdims=True))
    weights = jnp.exp(scores - top)
    total = lax.optimization_barrier(jnp.sum(weights, axis=-1))
    rounded = weights.astype(jnp.bfloat16).astype(jnp.float32)
    mixed = jnp.einsum('whij,wjhc->wihc', rounded, v_four)
    mixed = mixed / jnp.transpose(total, (0, 2, 1))[..., None]
    return mixed.astype(jnp.bfloat16).reshape(count, WT, D)

def reference(tokens, qkv_weight, proj_weight, up_weight, down_weight, pos_bias, class_bias, surface_class):
    nlat = tokens.shape[1]
    nlon = tokens.shape[2]
    tall = nlat + 8
    windows_tall = tall // 8
    rolled = jnp.roll(tokens, 4, axis=2)
    padded = jnp.pad(rolled, ((0, 0), (4, 4), (0, 0), (0, 0)))
    class_padded = jnp.pad(jnp.roll(surface_class, 4, axis=1), ((4, 4), (0, 0)))
    rows_global = jnp.arange(tall, dtype=jnp.int32) - 4
    inside = (rows_global >= 0) & (rows_global < nlat)
    bias_pos = pos_bias.astype(jnp.float32)
    table = class_bias.astype(jnp.float32)

    def windows(grid):
        return jnp.transpose(grid.reshape(LEV, windows_tall, 8, 8, -1), (1, 0, 2, 3, 4)).reshape(windows_tall, WT, -1)

    def one_column(index):
        block = lax.dynamic_slice_in_dim(padded, index * 8, 8, 2)
        class_block = lax.dynamic_slice_in_dim(class_padded, index * 8, 8, 1)
        normed = layer_norm(block.astype(jnp.float32)).astype(jnp.bfloat16)
        flat = windows(normed).reshape(-1, D)
        query = jnp.dot(flat, qkv_weight[0], preferred_element_type=jnp.float32).astype(jnp.bfloat16)
        keys = jnp.dot(flat, qkv_weight[1], preferred_element_type=jnp.float32).astype(jnp.bfloat16)
        values = jnp.dot(flat, qkv_weight[2], preferred_element_type=jnp.float32).astype(jnp.bfloat16)
        query_class = windows(jnp.broadcast_to(class_block[None, :, :, None], (LEV, tall, 8, 1)))[..., 0]
        allowed = windows(jnp.broadcast_to(inside[None, :, None, None], (LEV, tall, 8, 1)))[..., 0]
        bias = jnp.transpose(table[query_class], (0, 2, 1, 3)) + bias_pos[None]
        shape = (windows_tall, WT, D)
        mixed = attend(query.reshape(shape), keys.reshape(shape), values.reshape(shape), bias, allowed)
        projected = jnp.dot(mixed.reshape(-1, D), proj_weight, preferred_element_type=jnp.float32)
        grid = jnp.transpose(projected.reshape(windows_tall, LEV, 8, 8, D), (1, 0, 2, 3, 4)).reshape(LEV, tall, 8, D)
        grid = grid[:, 4:4 + nlat]
        hidden = (block[:, 4:4 + nlat].astype(jnp.float32) + grid).astype(jnp.bfloat16)
        normed_two = layer_norm(hidden.astype(jnp.float32)).astype(jnp.bfloat16)
        lifted = jnp.dot(normed_two, up_weight, preferred_element_type=jnp.float32)
        activated = jax.nn.gelu(lifted, approximate=False).astype(jnp.bfloat16)
        lowered = jnp.dot(activated, down_weight, preferred_element_type=jnp.float32)
        return (hidden.astype(jnp.float32) + lowered).astype(jnp.bfloat16)
    columns = lax.map(one_column, jnp.arange(nlon // 8, dtype=jnp.int32))
    joined = jnp.transpose(columns, (1, 2, 0, 3, 4)).reshape(LEV, nlat, nlon, D)
    return jnp.roll(joined, -4, axis=2)
```

```python
import jax
import jax.numpy as jnp
from jax import lax
from jax.experimental import pallas as pl
from jax.experimental.pallas import tpu as pltpu
from jax.sharding import PartitionSpec as P

BF = jnp.bfloat16
F32 = jnp.float32


def layer_norm(values):
    mean_value = jnp.mean(values, axis=-1, keepdims=True)
    centred = values - mean_value
    variance = jnp.mean(centred * centred, axis=-1, keepdims=True)
    return centred * lax.rsqrt(variance + 1e-05)


def window_order(lat):
    new = lax.broadcasted_iota(jnp.int32, (128, 128), 0)
    old = lax.broadcasted_iota(jnp.int32, (128, 128), 1)
    half = ((new >> 6) & 1) ^ lat
    level, patch = (new >> 5) & 1, (new >> 4) & 1
    row, column = (new >> 2) & 3, new & 3
    return (old == level * 64 + half * 32 + row * 8 + patch * 4 + column).astype(BF)


def prepare_bias(lat, pos_ref, class_ref, pos_scr, class_scr):
    order = window_order(lat)
    for h in range(pos_ref.shape[0]):
        rows = jnp.dot(order, pos_ref[h], preferred_element_type=F32).astype(BF)
        pos_scr[h] = lax.dot_general(
            rows, order, (((1,), (1,)), ((), ())), preferred_element_type=F32
        )
        class_scr[h] = lax.dot_general(
            order, class_ref[h], (((1,), (1,)), ((), ())), preferred_element_type=F32
        ).astype(BF)


def scores_of(q, k, bias):
    s = lax.dot_general(q, k, (((1,), (1,)), ((), ())), preferred_element_type=F32) + bias
    return jnp.exp(s - jnp.max(s, axis=-1, keepdims=True)).astype(BF)


def attend_pair(q, k, v, hot, pos_a, pos_b, class_a, class_b):
    low_q = lax.broadcasted_iota(jnp.int32, q.shape, 1) < 64
    low_k = lax.broadcasted_iota(jnp.int32, k.shape, 1) < 64
    zero = jnp.zeros_like(v)
    one = jnp.ones_like(v)
    p_a = scores_of(jnp.where(low_q, q, hot), jnp.where(low_k, k, class_a), pos_a)
    p_b = scores_of(jnp.where(low_q, hot, q), jnp.where(low_k, class_b, k), pos_b)
    v_a = jnp.concatenate([jnp.where(low_k, v, zero), jnp.where(low_k, one, zero)], axis=1)
    v_b = jnp.concatenate([jnp.where(low_k, zero, v), jnp.where(low_k, zero, one)], axis=1)
    if k.shape[0] == 128:
        out = jnp.dot(
            jnp.concatenate([p_a, p_b], axis=1),
            jnp.concatenate([v_a, v_b], axis=0),
            preferred_element_type=F32,
        )
    else:
        out = jnp.dot(p_a, v_a, preferred_element_type=F32) + jnp.dot(
            p_b, v_b, preferred_element_type=F32
        )
    return (out[:, :128] / out[:, 128:]).astype(BF)


def attend_column(w, q_scr, k_scr, v_scr, hot_ref, pos_scr, class_scr, store):
    def rows(ref, slots, lanes):
        parts = [ref[s, w, :, lanes] for s in slots]
        return parts[0] if len(parts) == 1 else jnp.concatenate(parts, axis=0)

    everything = slice(None)
    for pair in range(q_scr.shape[-1] // 128):
        lanes = slice(pair * 128, pair * 128 + 128)
        for q_slots, k_slots, q_part, k_part in (
            ((1, 2), (1, 2), everything, everything),
            ((3,), (3, 4), slice(0, 64), everything),
            ((0,), (0,), slice(64, 128), slice(64, 128)),
        ):
            mixed = attend_pair(
                rows(q_scr, q_slots, lanes),
                rows(k_scr, k_slots, lanes),
                rows(v_scr, k_slots, lanes),
                rows(hot_ref, q_slots, everything),
                pos_scr[2 * pair, q_part, k_part],
                pos_scr[2 * pair + 1, q_part, k_part],
                class_scr[2 * pair, k_part],
                class_scr[2 * pair + 1, k_part],
            )
            for at, slot in enumerate(q_slots):
                store(slot, lanes, mixed[at * 64 : at * 64 + 64])


def attention_kernel(
    x_ref, hot_ref, w_ref, pos_ref, class_ref, out_ref, q_scr, k_scr, v_scr, pos_scr, class_scr
):
    slots, columns, tall, width = x_ref.shape
    inner = w_ref.shape[-1]
    prepare_bias(lax.axis_index("lat"), pos_ref, class_ref, pos_scr, class_scr)

    @pl.loop(0, slots)
    def _(s):
        x = x_ref[s].reshape(columns * tall, width)
        normed = layer_norm(x.astype(F32)).astype(BF)

        def project(i):
            got = jnp.dot(normed, w_ref[i], preferred_element_type=F32).astype(BF)
            return got.reshape(columns, tall, inner)

        q_scr[s] = project(0) * jnp.asarray(0.125, BF)
        k_scr[s] = project(1)
        v_scr[s] = project(2)

    @pl.loop(0, columns)
    def _(w):
        def store(slot, lanes, block):
            for level in range(2):
                for side in range(2):
                    at = level * 32 + side * 16
                    out_ref[level, slot, 2 * w + side, :, lanes] = block[at : at + 16]

        attend_column(w, q_scr, k_scr, v_scr, hot_ref, pos_scr, class_scr, store)


def feed_kernel(
    x_ref, att_ref, proj_ref, up_ref, down_ref, keep_ref, send_ref
):
    me = lax.axis_index("tp")
    rows = x_ref.shape[1]
    step = 256

    def chunk(level, at):
        here = pl.ds(pl.multiple_of(at * step, step), step)
        share = jnp.dot(
            att_ref[0, level, here], proj_ref[0], preferred_element_type=F32
        ) + jnp.dot(att_ref[1, level, here], proj_ref[1], preferred_element_type=F32)
        hidden = (x_ref[level, here].astype(F32) + share).astype(BF)
        wide = hidden.astype(F32)
        normed = layer_norm(wide).astype(BF)
        lifted = jnp.dot(normed, up_ref[...], preferred_element_type=F32)
        active = (0.5 * lifted * (1.0 + lax.erf(lifted * (0.5**0.5)))).astype(BF)
        return here, wide, jnp.dot(active, down_ref[...], preferred_element_type=F32)

    @pl.loop(0, rows // step)
    def _(at):
        here, _, part = chunk(1 - me, at)
        send_ref[here] = part.astype(BF)

    @pl.loop(0, rows // step)
    def _(at):
        here, wide, part = chunk(me, at)
        keep_ref[here] = wide + part


def around(block, axis, shift):
    count = lax.axis_size(axis)
    return lax.ppermute(block, axis, [(i, (i + shift) % count) for i in range(count)])


def whole_vmem(n):
    return [pl.BlockSpec(memory_space=pltpu.VMEM)] * n


def body(
    tokens, qkv_weight, proj_weight, up_weight, down_weight, pos_bias, class_bias, surface_class
):
    heads = pos_bias.shape[0]
    _, tall, broad, width = tokens.shape
    inner = qkv_weight.shape[-1]
    lat = lax.axis_index("lat")
    slots, patches = tall // 4, broad // 4
    columns = patches // 2 + 1

    def mirrored(grid, axis):
        return jnp.where(lat == 1, jnp.flip(grid, axis), grid)

    own = tokens.reshape(slots, 4, patches, 4, width)
    own = jnp.transpose(own, (0, 2, 1, 3, 4)).reshape(slots, patches, 16, width)
    own = mirrored(own, 0)
    both = lax.all_gather(own, "tp", axis=0, tiled=False)
    west = around(both[:, :, -1:], "lon", 1)
    east = around(both[:, :, :1], "lon", -1)
    wide = jnp.concatenate([west, both, east], axis=2)
    beyond = around(wide[:, -1:], "lat", 1)
    grid = jnp.concatenate([wide, beyond], axis=1)
    grid = grid.reshape(2, slots + 1, columns, 2, 16, width)
    grid = jnp.transpose(grid, (1, 2, 0, 3, 4, 5)).reshape(slots + 1, columns, 64, width)

    cls = jnp.pad(surface_class, ((0, 0), (4, 4))).reshape(slots, 4, columns * 2, 4)
    cls = mirrored(jnp.transpose(cls, (0, 2, 1, 3)), 0).reshape(slots, columns, 1, 2, 16)
    cls = jnp.broadcast_to(cls, (slots, columns, 2, 2, 16)).reshape(slots, columns, 64, 1)
    hot = (cls == jnp.arange(128, dtype=jnp.int32) % 64).astype(BF)
    table = jnp.transpose(class_bias, (1, 0, 2))
    classes = table.shape[1]
    table = jnp.stack(
        [
            jnp.pad(table[0::2], ((0, 0), (64, 64 - classes), (0, 0))),
            jnp.pad(table[1::2], ((0, 0), (0, 128 - classes), (0, 0))),
        ],
        axis=1,
    ).reshape(heads, 128, 128)

    attended = pl.pallas_call(
        attention_kernel,
        out_shape=jax.ShapeDtypeStruct((2, slots, 2 * columns, 16, inner), BF),
        in_specs=whole_vmem(5),
        out_specs=whole_vmem(1)[0],
        scratch_shapes=[
            pltpu.VMEM((slots + 1, columns, 64, inner), BF),
            pltpu.VMEM((slots + 1, columns, 64, inner), BF),
            pltpu.VMEM((slots + 1, columns, 64, inner), BF),
            pltpu.VMEM((heads, 128, 128), F32),
            pltpu.VMEM((heads, 128, 128), BF),
        ],
        compiler_params=pltpu.CompilerParams(vmem_limit_bytes=56 * 2**20),
        name="window_attention",
    )(grid, hot, qkv_weight, pos_bias, table)

    attended = attended[:, :, 1:-1].reshape(2, tall * broad, inner)
    attended = lax.all_gather(attended, "tp", axis=0, tiled=False)
    proj = lax.all_gather(proj_weight, "tp", axis=0, tiled=False)
    keep, send = pl.pallas_call(
        feed_kernel,
        out_shape=(
            jax.ShapeDtypeStruct((tall * broad, width), F32),
            jax.ShapeDtypeStruct((tall * broad, width), BF),
        ),
        in_specs=whole_vmem(5),
        out_specs=tuple(whole_vmem(2)),
        compiler_params=pltpu.CompilerParams(vmem_limit_bytes=56 * 2**20),
        name="project_and_feed",
    )(both.reshape(2, tall * broad, width), attended, proj, up_weight, down_weight)
    got = around(send, "tp", 1)
    out = (keep + got.astype(F32)).astype(BF).reshape(slots, patches, 4, 4, width)
    out = mirrored(out, 0)
    return jnp.transpose(out, (0, 2, 1, 3, 4)).reshape(1, tall, broad, width)


def solution(mesh):
    placed = (
        P("tp", "lat", "lon", None),
        P(None, None, "tp"),
        P("tp", None),
        P(None, "tp"),
        P("tp", None),
        P("tp", None, None),
        P(None, "tp", None),
        P("lat", "lon"),
    )
    return jax.shard_map(
        body, mesh=mesh, in_specs=placed, out_specs=P("tp", "lat", "lon", None), check_vma=False
    )
```

```python
import jax
import jax.numpy as jnp
from jax import lax
from jax.experimental import pallas as pl
from jax.experimental.pallas import tpu as pltpu
from jax.sharding import PartitionSpec as P

BF = jnp.bfloat16
F32 = jnp.float32


def layer_norm(values):
    mean_value = jnp.mean(values, axis=-1, keepdims=True)
    centred = values - mean_value
    variance = jnp.mean(centred * centred, axis=-1, keepdims=True)
    return centred * lax.rsqrt(variance + 1e-05)


def window_order(lat):
    new = lax.broadcasted_iota(jnp.int32, (128, 128), 0)
    old = lax.broadcasted_iota(jnp.int32, (128, 128), 1)
    half = ((new >> 6) & 1) ^ lat
    level, patch = (new >> 5) & 1, (new >> 4) & 1
    row, column = (new >> 2) & 3, new & 3
    return (old == level * 64 + half * 32 + row * 8 + patch * 4 + column).astype(BF)


def prepare_bias(lat, pos_ref, class_ref, pos_scr, class_scr):
    order = window_order(lat)
    classes = class_ref.shape[1]
    for h in range(pos_ref.shape[0]):
        rows = jnp.dot(order, pos_ref[h], preferred_element_type=F32).astype(BF)
        pos_scr[h] = lax.dot_general(
            rows, order, (((1,), (1,)), ((), ())), preferred_element_type=F32
        )
        ahead = 64 if h % 2 == 0 else 0
        parts = [class_ref[h], jnp.zeros((128 - ahead - classes, 128), F32)]
        if ahead:
            parts = [jnp.zeros((ahead, 128), F32)] + parts
        table = jnp.concatenate(parts, axis=0).astype(BF)
        class_scr[h] = lax.dot_general(
            order, table, (((1,), (1,)), ((), ())), preferred_element_type=F32
        ).astype(BF)


def scores_of(q, k, bias):
    s = lax.dot_general(q, k, (((1,), (1,)), ((), ())), preferred_element_type=F32) + bias
    return jnp.exp(s - jnp.max(s, axis=-1, keepdims=True)).astype(BF)


def attend_pair(q, k, v, hot, pos_a, pos_b, class_a, class_b):
    low_q = lax.broadcasted_iota(jnp.int32, q.shape, 1) < 64
    low_k = lax.broadcasted_iota(jnp.int32, k.shape, 1) < 64
    zero = jnp.zeros_like(v)
    one = jnp.ones_like(v)
    p_a = scores_of(jnp.where(low_q, q, hot), jnp.where(low_k, k, class_a), pos_a)
    p_b = scores_of(jnp.where(low_q, hot, q), jnp.where(low_k, class_b, k), pos_b)
    v_a = jnp.concatenate([jnp.where(low_k, v, zero), jnp.where(low_k, one, zero)], axis=1)
    v_b = jnp.concatenate([jnp.where(low_k, zero, v), jnp.where(low_k, zero, one)], axis=1)
    if k.shape[0] == 128:
        out = jnp.dot(
            jnp.concatenate([p_a, p_b], axis=1),
            jnp.concatenate([v_a, v_b], axis=0),
            preferred_element_type=F32,
        )
    else:
        out = jnp.dot(p_a, v_a, preferred_element_type=F32) + jnp.dot(
            p_b, v_b, preferred_element_type=F32
        )
    return (out[:, :128] / out[:, 128:]).astype(BF)


def band_order(broad):
    size = 4 * broad
    new = lax.broadcasted_iota(jnp.int32, (size, size), 0)
    old = lax.broadcasted_iota(jnp.int32, (size, size), 1)
    return (old == ((new // 4) % 4) * broad + (new // 16) * 4 + new % 4).astype(BF)


WINDOWS = (
    ((1, 2), (1, 2), slice(None), slice(None)),
    ((0,), (0,), slice(64, 128), slice(64, 128)),
    ((3,), (3, 4), slice(0, 64), slice(None)),
)


def layer_kernel(
    tok_ref, cell_ref, pos_ref, class_ref, qkv_hbm, proj_hbm, up_hbm, down_hbm, out_ref,
    x, q_scr, k_scr, v_scr, hot, pos_scr, class_scr, att, keep, send, recv,
    qkv_ref, proj_ref, up_ref, down_ref, local_sem, send_sem, recv_sem,
):
    bands, size, width = tok_ref.shape
    patches = size // 16
    inner = att.shape[-1]
    lon, lat, me = lax.axis_index("lon"), lax.axis_index("lat"), lax.axis_index("tp")
    lons = lax.axis_size("lon")
    other, across = 1 - me, 1 - lat
    east, west = lax.rem(lon + 1, lons), lax.rem(lon + lons - 1, lons)
    peer = (lon, lat, other)

    loads = [pltpu.make_async_copy(qkv_hbm.at[i], qkv_ref.at[i], local_sem.at[i]) for i in range(3)]
    loads += [
        pltpu.make_async_copy(proj_hbm, proj_ref.at[me], local_sem.at[3]),
        pltpu.make_async_copy(up_hbm, up_ref, local_sem.at[4]),
        pltpu.make_async_copy(down_hbm, down_ref, local_sem.at[5]),
    ]
    for load in loads:
        load.start()

    friends = [peer]
    for core in (me, other):
        friends += [(east, lat, core), (west, lat, core), (lon, across, core)]
        friends += [(east, across, core), (west, across, core)]
    barrier = pltpu.get_barrier_semaphore()
    for friend in friends:
        pl.semaphore_signal(
            barrier, inc=1, device_id=friend, device_id_type=pl.DeviceIdType.MESH
        )

    order = band_order(size // 4)

    @pl.loop(0, bands)
    def _(s):
        row = jnp.where(lat == 1, bands - 1 - s, s)
        moved = jnp.dot(order, tok_ref[row], preferred_element_type=F32).astype(BF)
        x[me, s, 1 : patches + 1] = moved.reshape(patches, 16, width)

    pl.semaphore_wait(barrier, len(friends))
    count = 0

    def remote(source, target, device):
        nonlocal count
        copy = pltpu.make_async_remote_copy(
            src_ref=source,
            dst_ref=target,
            send_sem=send_sem.at[count],
            recv_sem=recv_sem.at[count],
            device_id=device,
            device_id_type=pl.DeviceIdType.MESH,
        )
        count += 1
        return copy

    mine = x.at[me, 0:bands, 1 : patches + 1]
    twin = [remote(mine, mine, peer)]
    sides, beyond = [], []
    for core in (me, other):
        sides.append(remote(x.at[me, 0:bands, patches], x.at[me, 0:bands, 0], (east, lat, core)))
        sides.append(remote(x.at[me, 0:bands, 1], x.at[me, 0:bands, patches + 1], (west, lat, core)))
    for core in (me, other):
        inside = slice(1, patches + 1)
        beyond.append(
            remote(x.at[me, bands - 1, inside], x.at[me, bands, inside], (lon, across, core))
        )
        beyond.append(
            remote(x.at[me, bands - 1, patches], x.at[me, bands, 0], (east, across, core))
        )
        beyond.append(
            remote(x.at[me, bands - 1, 1], x.at[me, bands, patches + 1], (west, across, core))
        )
    projs = [remote(proj_hbm, proj_ref.at[me], peer)]
    for copy in twin + sides + beyond + projs:
        copy.start()

    prepare_bias(lat, pos_ref, class_ref, pos_scr, class_scr)

    @pl.loop(0, bands)
    def _(s):
        row = jnp.where(lat == 1, bands - 1 - s, s)
        lane = lax.broadcasted_iota(jnp.int32, (128, size), 0) % 64
        flags = (lane == cell_ref[row]).astype(F32).astype(BF)
        block = lax.dot_general(
            order, flags, (((1,), (1,)), ((), ())), preferred_element_type=F32
        ).astype(BF)
        for level in range(2):
            hot[s, level, 1 : patches + 1] = block.reshape(patches, 16, 128)

    def normal(rows):
        return layer_norm(rows.astype(F32)).astype(BF)

    def project(normed, i):
        return jnp.dot(normed, qkv_ref[i], preferred_element_type=F32).astype(BF)

    def project_level(level):
        @pl.loop(0, bands)
        def _(s):
            normed = normal(x[level, s, 1 : patches + 1].reshape(size, width))
            for i, ref in enumerate((q_scr, k_scr, v_scr)):
                got = project(normed, i)
                if i == 0:
                    got = got * jnp.asarray(0.125, BF)
                ref[s, level, 1 : patches + 1] = got.reshape(patches, 16, inner)

    for load in loads[:3]:
        load.wait()
    project_level(me)
    twin[0].wait_recv()
    project_level(other)
    for copy in sides:
        copy.wait_recv()

    @pl.loop(0, 2)
    def _(level):
        half = bands * 16
        rows = jnp.concatenate(
            [
                x[level, 0:bands, 0].reshape(half, width),
                x[level, 0:bands, patches + 1].reshape(half, width),
            ],
            axis=0,
        )
        normed = normal(rows)
        for i, ref in ((1, k_scr), (2, v_scr)):
            got = project(normed, i)
            ref[0:bands, level, 0] = got[:half].reshape(bands, 16, inner)
            ref[0:bands, level, patches + 1] = got[half:].reshape(bands, 16, inner)

    def attend_windows(windows):
        @pl.loop(0, patches // 2 + 1)
        def _(w):
            def rows(ref, slots, lanes):
                parts = [ref[s, :, pl.ds(2 * w, 2), :, lanes].reshape(64, 128) for s in slots]
                return parts[0] if len(parts) == 1 else jnp.concatenate(parts, axis=0)

            for pair in range(inner // 128):
                lanes = slice(pair * 128, pair * 128 + 128)
                for q_slots, k_slots, q_part, k_part in windows:
                    mixed = attend_pair(
                        rows(q_scr, q_slots, lanes),
                        rows(k_scr, k_slots, lanes),
                        rows(v_scr, k_slots, lanes),
                        rows(hot, q_slots, slice(None)),
                        pos_scr[2 * pair, q_part, k_part],
                        pos_scr[2 * pair + 1, q_part, k_part],
                        class_scr[2 * pair, k_part],
                        class_scr[2 * pair + 1, k_part],
                    )
                    for at, slot in enumerate(q_slots):
                        block = mixed[at * 64 : at * 64 + 64].reshape(2, 2, 16, 128)
                        att[me, slot, :, pl.ds(2 * w, 2), :, lanes] = block

    def share(first, last):
        part = att.at[me, first:last, :, 1 : patches + 1]
        copy = remote(part, part, peer)
        copy.start()
        return copy

    attend_windows(WINDOWS[:2])
    early = share(0, bands - 1)
    for copy in beyond:
        copy.wait_recv()

    @pl.loop(0, 2)
    def _(level):
        normed = normal(x[level, bands].reshape(size + 32, width))
        for i, ref in ((1, k_scr), (2, v_scr)):
            ref[bands, level] = project(normed, i).reshape(patches + 2, 16, inner)

    attend_windows(WINDOWS[2:])
    late = share(bands - 1, bands)
    for load in loads[3:]:
        load.wait()
    projs[0].wait_recv()
    early.wait_recv()
    pieces = 4
    hidden_units = up_ref.shape[1] // pieces

    def feed(level, at):
        slots = pl.ds(2 * at, 2)
        wide = x[level, slots, 1 : patches + 1].reshape(2 * size, width).astype(F32)
        for half in range(2):
            mixed = att[half, slots, level, 1 : patches + 1].reshape(2 * size, inner)
            if half == 0:
                total = jnp.dot(mixed, proj_ref[half], preferred_element_type=F32)
            else:
                total += jnp.dot(mixed, proj_ref[half], preferred_element_type=F32)
        wide = (wide + total).astype(BF).astype(F32)
        normed = normal(wide)
        total = None
        for piece in range(pieces):
            units = slice(piece * hidden_units, (piece + 1) * hidden_units)
            lifted = jnp.dot(normed, up_ref[:, units], preferred_element_type=F32)
            active = (0.5 * lifted * (1.0 + lax.erf(lifted * (0.5**0.5)))).astype(BF)
            part = jnp.dot(active, down_ref[units], preferred_element_type=F32)
            total = part if total is None else total + part
        return wide, total

    steps = bands // 2
    returns = [remote(send.at[at], recv.at[at], peer) for at in range(steps)]
    for at in range(steps):
        if at == steps - 1:
            late.wait_recv()
        _, total = feed(other, at)
        send[at] = total.astype(BF)
        returns[at].start()

    @pl.loop(0, steps)
    def _(at):
        wide, total = feed(me, at)
        keep[at] = wide + total

    for at in range(steps):
        returns[at].wait_recv()
    back = band_order(size // 4)

    @pl.loop(0, bands)
    def _(s):
        row = jnp.where(lat == 1, bands - 1 - s, s)
        at, here = s // 2, pl.ds((s % 2) * size, size)
        done = (keep[at, here] + recv[at, here].astype(F32)).astype(BF)
        out_ref[row] = lax.dot_general(
            back, done, (((0,), (0,)), ((), ())), preferred_element_type=F32
        ).astype(BF)

    for copy in twin + sides + beyond + projs + [early, late] + returns:
        copy.wait_send()


def body(
    tokens, qkv_weight, proj_weight, up_weight, down_weight, pos_bias, class_bias, surface_class
):
    heads = pos_bias.shape[0]
    _, tall, broad, width = tokens.shape
    inner, units = qkv_weight.shape[-1], up_weight.shape[-1]
    bands, patches, size = tall // 4, broad // 4, 4 * broad
    copies = 1 + 4 + 6 + 1 + 2 + bands // 2
    vmem = pl.BlockSpec(memory_space=pltpu.VMEM)
    anywhere = pl.BlockSpec(memory_space=pl.ANY)
    scratch = (
        ((2, bands + 1, patches + 2, 16, width), BF),
        ((bands, 2, patches + 2, 16, inner), BF),
        ((bands + 1, 2, patches + 2, 16, inner), BF),
        ((bands + 1, 2, patches + 2, 16, inner), BF),
        ((bands, 2, patches + 2, 16, 128), BF),
        ((heads, 128, 128), F32),
        ((heads, 128, 128), BF),
        ((2, bands, 2, patches + 2, 16, inner), BF),
        ((bands // 2, 2 * size, width), F32),
        ((bands // 2, 2 * size, width), BF),
        ((bands // 2, 2 * size, width), BF),
        (qkv_weight.shape, BF),
        ((2,) + proj_weight.shape, BF),
        (up_weight.shape, BF),
        (down_weight.shape, BF),
    )
    out = pl.pallas_call(
        layer_kernel,
        out_shape=jax.ShapeDtypeStruct((bands, size, width), BF),
        in_specs=[vmem] * 4 + [anywhere] * 4,
        out_specs=vmem,
        scratch_shapes=[pltpu.VMEM(shape, kind) for shape, kind in scratch]
        + [
            pltpu.SemaphoreType.DMA((6,)),
            pltpu.SemaphoreType.DMA((copies,)),
            pltpu.SemaphoreType.DMA((copies,)),
        ],
        compiler_params=pltpu.CompilerParams(
            collective_id=0, has_side_effects=True, vmem_limit_bytes=58 * 2**20
        ),
        cost_estimate=pl.CostEstimate(
            flops=17 * 10**9, bytes_accessed=16 * 2**20, transcendentals=4 * 10**6
        ),
        name="window_layer",
    )(
        tokens.reshape(bands, size, width),
        surface_class.reshape(bands, 1, size),
        pos_bias,
        jnp.transpose(class_bias, (1, 0, 2)).astype(F32),
        qkv_weight,
        proj_weight,
        up_weight,
        down_weight,
    )
    return out.reshape(1, tall, broad, width)


def solution(mesh):
    placed = (
        P("tp", "lat", "lon", None),
        P(None, None, "tp"),
        P("tp", None),
        P(None, "tp"),
        P("tp", None),
        P("tp", None, None),
        P(None, "tp", None),
        P("lat", "lon"),
    )
    return jax.shard_map(
        body, mesh=mesh, in_specs=placed, out_specs=P("tp", "lat", "lon", None), check_vma=False
    )
```

```python
import jax
import jax.numpy as jnp
from jax import lax
from jax.experimental import pallas as pl
from jax.experimental.pallas import tpu as pltpu
from jax.sharding import PartitionSpec as P

BF = jnp.bfloat16
F32 = jnp.float32


def layer_norm(values):
    mean_value = jnp.mean(values, axis=-1, keepdims=True)
    centred = values - mean_value
    variance = jnp.mean(centred * centred, axis=-1, keepdims=True)
    return centred * lax.rsqrt(variance + 1e-05)


def window_order(lat):
    new = lax.broadcasted_iota(jnp.int32, (128, 128), 0)
    old = lax.broadcasted_iota(jnp.int32, (128, 128), 1)
    half = ((new >> 6) & 1) ^ lat
    level, patch = (new >> 5) & 1, (new >> 4) & 1
    row, column = (new >> 2) & 3, new & 3
    return (old == level * 64 + half * 32 + row * 8 + patch * 4 + column).astype(BF)


def prepare_bias(lat, pos_ref, class_ref, pos_scr, class_scr):
    order = window_order(lat)
    classes, heads, keys = class_ref.shape
    flat = class_ref[...].astype(F32).reshape(classes * heads, keys).astype(BF)
    flat = lax.dot_general(
        order, flat, (((1,), (1,)), ((), ())), preferred_element_type=F32
    ).astype(BF)
    entry = lax.broadcasted_iota(jnp.int32, (classes * heads, 128), 0)
    lane = lax.broadcasted_iota(jnp.int32, (classes * heads, 128), 1)
    for h in range(heads):
        rows = jnp.dot(order, pos_ref[h], preferred_element_type=F32).astype(BF)
        pos_scr[h] = lax.dot_general(
            rows, order, (((1,), (1,)), ((), ())), preferred_element_type=F32
        )
        ahead = 64 if h % 2 == 0 else 0
        pick = (entry == (lane - ahead) * heads + h).astype(F32).astype(BF)
        class_scr[h] = jnp.dot(flat, pick, preferred_element_type=F32).astype(BF)


def scores_of(q, k, bias):
    s = lax.dot_general(q, k, (((1,), (1,)), ((), ())), preferred_element_type=F32) + bias
    return jnp.exp(s - jnp.max(s, axis=-1, keepdims=True)).astype(BF)


def attend_pair(q, k, v, hot, pos_a, pos_b, class_a, class_b):
    low_q = lax.broadcasted_iota(jnp.int32, q.shape, 1) < 64
    low_k = lax.broadcasted_iota(jnp.int32, k.shape, 1) < 64
    zero = jnp.zeros_like(v)
    one = jnp.ones_like(v)
    p_a = scores_of(jnp.where(low_q, q, hot), jnp.where(low_k, k, class_a), pos_a)
    p_b = scores_of(jnp.where(low_q, hot, q), jnp.where(low_k, class_b, k), pos_b)
    v_a = jnp.concatenate([jnp.where(low_k, v, zero), jnp.where(low_k, one, zero)], axis=1)
    v_b = jnp.concatenate([jnp.where(low_k, zero, v), jnp.where(low_k, zero, one)], axis=1)
    if k.shape[0] == 128:
        out = jnp.dot(
            jnp.concatenate([p_a, p_b], axis=1),
            jnp.concatenate([v_a, v_b], axis=0),
            preferred_element_type=F32,
        )
    else:
        out = jnp.dot(p_a, v_a, preferred_element_type=F32) + jnp.dot(
            p_b, v_b, preferred_element_type=F32
        )
    return (out[:, :128] / out[:, 128:]).astype(BF)


def band_order(broad):
    size = 4 * broad
    new = lax.broadcasted_iota(jnp.int32, (size, size), 0)
    old = lax.broadcasted_iota(jnp.int32, (size, size), 1)
    return (old == ((new // 4) % 4) * broad + (new // 16) * 4 + new % 4).astype(BF)


WINDOWS = (
    ((1, 2), (1, 2), slice(None), slice(None)),
    ((0,), (0,), slice(64, 128), slice(64, 128)),
    ((3,), (3, 4), slice(0, 64), slice(None)),
)


def layer_kernel(
    tok_ref, cell_ref, pos_ref, class_ref, qkv_hbm, proj_hbm, up_hbm, down_hbm, out_ref,
    x, q_scr, k_scr, v_scr, hot, pos_scr, class_scr, att, keep, send, recv,
    qkv_ref, proj_ref, up_ref, down_ref, local_sem, send_sem, recv_sem,
):
    bands, size, width = tok_ref.shape
    patches = size // 16
    inner = att.shape[-1]
    lon, lat, me = lax.axis_index("lon"), lax.axis_index("lat"), lax.axis_index("tp")
    lons = lax.axis_size("lon")
    other, across = 1 - me, 1 - lat
    east, west = lax.rem(lon + 1, lons), lax.rem(lon + lons - 1, lons)
    peer = (lon, lat, other)

    loads = [pltpu.make_async_copy(qkv_hbm.at[i], qkv_ref.at[i], local_sem.at[i]) for i in range(3)]
    loads += [
        pltpu.make_async_copy(proj_hbm, proj_ref.at[me], local_sem.at[3]),
        pltpu.make_async_copy(up_hbm, up_ref, local_sem.at[4]),
        pltpu.make_async_copy(down_hbm, down_ref, local_sem.at[5]),
    ]
    for load in loads:
        load.start()

    friends = [peer]
    for core in (me, other):
        friends += [(east, lat, core), (west, lat, core), (lon, across, core)]
        friends += [(east, across, core), (west, across, core)]
    barrier = pltpu.get_barrier_semaphore()
    for friend in friends:
        pl.semaphore_signal(
            barrier, inc=1, device_id=friend, device_id_type=pl.DeviceIdType.MESH
        )

    order = band_order(size // 4)

    @pl.loop(0, bands)
    def _(s):
        row = jnp.where(lat == 1, bands - 1 - s, s)
        moved = jnp.dot(order, tok_ref[row], preferred_element_type=F32).astype(BF)
        x[me, s, 1 : patches + 1] = moved.reshape(patches, 16, width)

    pl.semaphore_wait(barrier, len(friends))
    count = 0

    def remote(source, target, device):
        nonlocal count
        copy = pltpu.make_async_remote_copy(
            src_ref=source,
            dst_ref=target,
            send_sem=send_sem.at[count],
            recv_sem=recv_sem.at[count],
            device_id=device,
            device_id_type=pl.DeviceIdType.MESH,
        )
        count += 1
        return copy

    mine = x.at[me, 0:bands, 1 : patches + 1]
    twin = [remote(mine, mine, peer)]
    sides, beyond = [], []
    for core in (me, other):
        sides.append(remote(x.at[me, 0:bands, patches], x.at[me, 0:bands, 0], (east, lat, core)))
        sides.append(remote(x.at[me, 0:bands, 1], x.at[me, 0:bands, patches + 1], (west, lat, core)))
    for core in (me, other):
        inside = slice(1, patches + 1)
        beyond.append(
            remote(x.at[me, bands - 1, inside], x.at[me, bands, inside], (lon, across, core))
        )
        beyond.append(
            remote(x.at[me, bands - 1, patches], x.at[me, bands, 0], (east, across, core))
        )
        beyond.append(
            remote(x.at[me, bands - 1, 1], x.at[me, bands, patches + 1], (west, across, core))
        )
    projs = [remote(proj_hbm, proj_ref.at[me], peer)]
    for copy in twin + sides + beyond + projs:
        copy.start()

    prepare_bias(lat, pos_ref, class_ref, pos_scr, class_scr)

    @pl.loop(0, bands)
    def _(s):
        row = jnp.where(lat == 1, bands - 1 - s, s)
        lane = lax.broadcasted_iota(jnp.int32, (128, size), 0) % 64
        cells = jnp.concatenate([cell_ref[pl.ds(4 * row + i, 1)] for i in range(4)], axis=1)
        flags = (lane == cells).astype(F32).astype(BF)
        block = lax.dot_general(
            order, flags, (((1,), (1,)), ((), ())), preferred_element_type=F32
        ).astype(BF)
        for level in range(2):
            hot[s, level, 1 : patches + 1] = block.reshape(patches, 16, 128)

    def normal(rows):
        return layer_norm(rows.astype(F32)).astype(BF)

    def project(normed, i):
        return jnp.dot(normed, qkv_ref[i], preferred_element_type=F32).astype(BF)

    def project_level(level):
        inside = slice(1, patches + 1)
        normed = normal(x[level, 0:bands, inside].reshape(bands * size, width))
        for i, ref in enumerate((q_scr, k_scr, v_scr)):
            got = project(normed, i)
            if i == 0:
                got = got * jnp.asarray(0.125, BF)
            ref[0:bands, level, inside] = got.reshape(bands, patches, 16, inner)

    for load in loads[:3]:
        load.wait()
    project_level(me)
    twin[0].wait_recv()
    project_level(other)
    def attend_windows(windows, places, first, stride):
        @pl.loop(0, places)
        def _(i):
            w = first + i * stride

            def rows(ref, slots, lanes):
                parts = [ref[s, :, pl.ds(2 * w, 2), :, lanes].reshape(64, 128) for s in slots]
                return parts[0] if len(parts) == 1 else jnp.concatenate(parts, axis=0)

            for pair in range(inner // 128):
                lanes = slice(pair * 128, pair * 128 + 128)
                for q_slots, k_slots, q_part, k_part in windows:
                    mixed = attend_pair(
                        rows(q_scr, q_slots, lanes),
                        rows(k_scr, k_slots, lanes),
                        rows(v_scr, k_slots, lanes),
                        rows(hot, q_slots, slice(None)),
                        pos_scr[2 * pair, q_part, k_part],
                        pos_scr[2 * pair + 1, q_part, k_part],
                        class_scr[2 * pair, k_part],
                        class_scr[2 * pair + 1, k_part],
                    )
                    for at, slot in enumerate(q_slots):
                        block = mixed[at * 64 : at * 64 + 64].reshape(2, 2, 16, 128)
                        att[me, slot, :, pl.ds(2 * w, 2), :, lanes] = block

    def share(first, last):
        part = att.at[me, first:last, :, 1 : patches + 1]
        copy = remote(part, part, peer)
        copy.start()
        return copy

    attend_windows(WINDOWS[:2], patches // 2 - 1, 1, 1)
    for copy in sides:
        copy.wait_recv()

    half = bands * 16
    ends = [(level, place) for level in range(2) for place in (0, patches + 1)]
    rows = [x[level, 0:bands, place].reshape(half, width) for level, place in ends]
    normed = normal(jnp.concatenate(rows, axis=0))
    for i, ref in ((1, k_scr), (2, v_scr)):
        got = project(normed, i)
        for at, (level, place) in enumerate(ends):
            part = got[at * half : at * half + half]
            ref[0:bands, level, place] = part.reshape(bands, 16, inner)

    attend_windows(WINDOWS[:2], 2, 0, patches // 2)
    early = share(0, bands - 1)
    for copy in beyond:
        copy.wait_recv()

    normed = normal(x[:, bands].reshape(2 * (size + 32), width))
    for i, ref in ((1, k_scr), (2, v_scr)):
        ref[bands] = project(normed, i).reshape(2, patches + 2, 16, inner)

    attend_windows(WINDOWS[2:], patches // 2 + 1, 0, 1)
    late = share(bands - 1, bands)
    for load in loads[3:]:
        load.wait()
    projs[0].wait_recv()
    early.wait_recv()
    pieces = 4
    group = send.shape[1] // size
    hidden_units = up_ref.shape[1] // pieces

    def feed(level, at):
        slots = slice(group * at, group * at + group)
        wide = x[level, slots, 1 : patches + 1].reshape(group * size, width).astype(F32)
        for half in range(2):
            mixed = att[half, slots, level, 1 : patches + 1].reshape(group * size, inner)
            if half == 0:
                total = jnp.dot(mixed, proj_ref[half], preferred_element_type=F32)
            else:
                total += jnp.dot(mixed, proj_ref[half], preferred_element_type=F32)
        wide = (wide + total).astype(BF).astype(F32)
        normed = normal(wide)
        total = None
        for piece in range(pieces):
            units = slice(piece * hidden_units, (piece + 1) * hidden_units)
            lifted = jnp.dot(normed, up_ref[:, units], preferred_element_type=F32)
            active = (0.5 * lifted * (1.0 + lax.erf(lifted * (0.5**0.5)))).astype(BF)
            part = jnp.dot(active, down_ref[units], preferred_element_type=F32)
            total = part if total is None else total + part
        return wide, total

    steps = bands // group
    returns = [remote(send.at[at], recv.at[at], peer) for at in range(steps)]
    for at in range(steps):
        if at == steps - 1:
            late.wait_recv()
        _, total = feed(other, at)
        send[at] = total.astype(BF)
        returns[at].start()

    back = band_order(size // 4)
    for at in range(steps):
        wide, total = feed(me, at)
        keep[...] = wide + total
        returns[at].wait_recv()
        for part in range(group):
            s = at * group + part
            row = jnp.where(lat == 1, bands - 1 - s, s)
            here = slice(part * size, (part + 1) * size)
            done = (keep[here] + recv[at, here].astype(F32)).astype(BF)
            out_ref[row] = lax.dot_general(
                back, done, (((0,), (0,)), ((), ())), preferred_element_type=F32
            ).astype(BF)

    for copy in twin + sides + beyond + projs + [early, late] + returns:
        copy.wait_send()


def body(
    tokens, qkv_weight, proj_weight, up_weight, down_weight, pos_bias, class_bias, surface_class
):
    heads = pos_bias.shape[0]
    _, tall, broad, width = tokens.shape
    inner, units = qkv_weight.shape[-1], up_weight.shape[-1]
    bands, patches, size = tall // 4, broad // 4, 4 * broad
    group = 4
    copies = 1 + 4 + 6 + 1 + 2 + bands // group
    vmem = pl.BlockSpec(memory_space=pltpu.VMEM)
    anywhere = pl.BlockSpec(memory_space=pl.ANY)
    scratch = (
        ((2, bands + 1, patches + 2, 16, width), BF),
        ((bands, 2, patches + 2, 16, inner), BF),
        ((bands + 1, 2, patches + 2, 16, inner), BF),
        ((bands + 1, 2, patches + 2, 16, inner), BF),
        ((bands, 2, patches + 2, 16, 128), BF),
        ((heads, 128, 128), F32),
        ((heads, 128, 128), BF),
        ((2, bands, 2, patches + 2, 16, inner), BF),
        ((group * size, width), F32),
        ((bands // group, group * size, width), BF),
        ((bands // group, group * size, width), BF),
        (qkv_weight.shape, BF),
        ((2,) + proj_weight.shape, BF),
        (up_weight.shape, BF),
        (down_weight.shape, BF),
    )
    out = pl.pallas_call(
        layer_kernel,
        out_shape=jax.ShapeDtypeStruct((bands, size, width), BF),
        in_specs=[vmem] * 4 + [anywhere] * 4,
        out_specs=vmem,
        scratch_shapes=[pltpu.VMEM(shape, kind) for shape, kind in scratch]
        + [
            pltpu.SemaphoreType.DMA((6,)),
            pltpu.SemaphoreType.DMA((copies,)),
            pltpu.SemaphoreType.DMA((copies,)),
        ],
        compiler_params=pltpu.CompilerParams(
            collective_id=0, has_side_effects=True, vmem_limit_bytes=58 * 2**20
        ),
        cost_estimate=pl.CostEstimate(
            flops=17 * 10**9, bytes_accessed=16 * 2**20, transcendentals=4 * 10**6
        ),
        name="window_layer",
    )(
        tokens.reshape(bands, size, width),
        surface_class,
        pos_bias,
        class_bias,
        qkv_weight,
        proj_weight,
        up_weight,
        down_weight,
    )
    return out.reshape(1, tall, broad, width)


def solution(mesh):
    placed = (
        P("tp", "lat", "lon", None),
        P(None, None, "tp"),
        P("tp", None),
        P(None, "tp"),
        P("tp", None),
        P("tp", None, None),
        P(None, "tp", None),
        P("lat", "lon"),
    )
    return jax.shard_map(
        body, mesh=mesh, in_specs=placed, out_specs=P("tp", "lat", "lon", None), check_vma=False
    )
```

```python
import jax
import jax.numpy as jnp
from jax import lax
from jax.experimental import pallas as pl
from jax.experimental.pallas import tpu as pltpu
from jax.sharding import PartitionSpec as P

BF = jnp.bfloat16
F32 = jnp.float32


def layer_norm(values):
    mean_value = jnp.mean(values, axis=-1, keepdims=True)
    centred = values - mean_value
    variance = jnp.mean(centred * centred, axis=-1, keepdims=True)
    return centred * lax.rsqrt(variance + 1e-05)


def window_order(lat):
    new = lax.broadcasted_iota(jnp.int32, (128, 128), 0)
    old = lax.broadcasted_iota(jnp.int32, (128, 128), 1)
    half = ((new >> 6) & 1) ^ lat
    level, patch = (new >> 5) & 1, (new >> 4) & 1
    row, column = (new >> 2) & 3, new & 3
    return (old == level * 64 + half * 32 + row * 8 + patch * 4 + column).astype(BF)


def prepare_bias(lat, pos_ref, class_ref, pos_scr, class_scr):
    order = window_order(lat)
    classes, heads, keys = class_ref.shape
    flat = class_ref[...].astype(F32).reshape(classes * heads, keys).astype(BF)
    flat = lax.dot_general(
        order, flat, (((1,), (1,)), ((), ())), preferred_element_type=F32
    ).astype(BF)
    entry = lax.broadcasted_iota(jnp.int32, (classes * heads, 128), 0)
    lane = lax.broadcasted_iota(jnp.int32, (classes * heads, 128), 1)
    for h in range(heads):
        rows = jnp.dot(order, pos_ref[h], preferred_element_type=F32).astype(BF)
        pos_scr[h] = lax.dot_general(
            rows, order, (((1,), (1,)), ((), ())), preferred_element_type=F32
        )
        ahead = 64 if h % 2 == 0 else 0
        pick = (entry == (lane - ahead) * heads + h).astype(F32).astype(BF)
        class_scr[h] = jnp.dot(flat, pick, preferred_element_type=F32).astype(BF)


def scores_of(q, k, bias):
    s = lax.dot_general(q, k, (((1,), (1,)), ((), ())), preferred_element_type=F32) + bias
    return jnp.exp(s - jnp.max(s, axis=-1, keepdims=True)).astype(BF)


def attend_pair(q, k, v, hot, pos_a, pos_b, class_a, class_b):
    low_q = lax.broadcasted_iota(jnp.int32, q.shape, 1) < 64
    low_k = lax.broadcasted_iota(jnp.int32, k.shape, 1) < 64
    zero = jnp.zeros_like(v)
    one = jnp.ones_like(v)
    p_a = scores_of(jnp.where(low_q, q, hot), jnp.where(low_k, k, class_a), pos_a)
    p_b = scores_of(jnp.where(low_q, hot, q), jnp.where(low_k, class_b, k), pos_b)
    v_a = jnp.concatenate([jnp.where(low_k, v, zero), jnp.where(low_k, one, zero)], axis=1)
    v_b = jnp.concatenate([jnp.where(low_k, zero, v), jnp.where(low_k, zero, one)], axis=1)
    if k.shape[0] == 128:
        out = jnp.dot(
            jnp.concatenate([p_a, p_b], axis=1),
            jnp.concatenate([v_a, v_b], axis=0),
            preferred_element_type=F32,
        )
    else:
        out = jnp.dot(p_a, v_a, preferred_element_type=F32) + jnp.dot(
            p_b, v_b, preferred_element_type=F32
        )
    return (out[:, :128] / out[:, 128:]).astype(BF)


def band_order(broad):
    size = 4 * broad
    new = lax.broadcasted_iota(jnp.int32, (size, size), 0)
    old = lax.broadcasted_iota(jnp.int32, (size, size), 1)
    return (old == ((new // 4) % 4) * broad + (new // 16) * 4 + new % 4).astype(BF)


WINDOWS = (
    ((1, 2), (1, 2), slice(None), slice(None)),
    ((0,), (0,), slice(64, 128), slice(64, 128)),
    ((3,), (3, 4), slice(0, 64), slice(None)),
)


def layer_kernel(
    tok_ref, cell_ref, pos_ref, class_ref, qkv_hbm, proj_hbm, up_hbm, down_hbm, out_ref,
    x, q_scr, k_scr, v_scr, hot, pos_scr, class_scr, att, keep, send, recv,
    qkv_ref, proj_ref, up_ref, down_ref, local_sem, send_sem, recv_sem,
):
    bands, size, width = tok_ref.shape
    patches = size // 16
    inner = att.shape[-1]
    lon, lat, me = lax.axis_index("lon"), lax.axis_index("lat"), lax.axis_index("tp")
    lons = lax.axis_size("lon")
    other, across = 1 - me, 1 - lat
    east, west = lax.rem(lon + 1, lons), lax.rem(lon + lons - 1, lons)
    peer = (lon, lat, other)

    loads = [pltpu.make_async_copy(qkv_hbm.at[i], qkv_ref.at[i], local_sem.at[i]) for i in range(3)]
    loads += [
        pltpu.make_async_copy(proj_hbm, proj_ref.at[me], local_sem.at[3]),
        pltpu.make_async_copy(up_hbm, up_ref, local_sem.at[4]),
        pltpu.make_async_copy(down_hbm, down_ref, local_sem.at[5]),
    ]
    for load in loads:
        load.start()

    friends = [peer]
    for core in (me, other):
        friends += [(east, lat, core), (west, lat, core), (lon, across, core)]
        friends += [(east, across, core), (west, across, core)]
    barrier = pltpu.get_barrier_semaphore()
    for friend in friends:
        pl.semaphore_signal(
            barrier, inc=1, device_id=friend, device_id_type=pl.DeviceIdType.MESH
        )

    order = band_order(size // 4)

    @pl.loop(0, bands)
    def _(s):
        row = jnp.where(lat == 1, bands - 1 - s, s)
        moved = jnp.dot(order, tok_ref[row], preferred_element_type=F32).astype(BF)
        x[me, s, 1 : patches + 1] = moved.reshape(patches, 16, width)

    pl.semaphore_wait(barrier, len(friends))
    count = 0

    def remote(source, target, device):
        nonlocal count
        copy = pltpu.make_async_remote_copy(
            src_ref=source,
            dst_ref=target,
            send_sem=send_sem.at[count],
            recv_sem=recv_sem.at[count],
            device_id=device,
            device_id_type=pl.DeviceIdType.MESH,
        )
        count += 1
        return copy

    mine = x.at[me, 0:bands, 1 : patches + 1]
    twin = [remote(mine, mine, peer)]
    sides, beyond = [], []
    for core in (me, other):
        sides.append(remote(x.at[me, 0:bands, patches], x.at[me, 0:bands, 0], (east, lat, core)))
        sides.append(remote(x.at[me, 0:bands, 1], x.at[me, 0:bands, patches + 1], (west, lat, core)))
    for core in (me, other):
        inside = slice(1, patches + 1)
        beyond.append(
            remote(x.at[me, bands - 1, inside], x.at[me, bands, inside], (lon, across, core))
        )
        beyond.append(
            remote(x.at[me, bands - 1, patches], x.at[me, bands, 0], (east, across, core))
        )
        beyond.append(
            remote(x.at[me, bands - 1, 1], x.at[me, bands, patches + 1], (west, across, core))
        )
    projs = [remote(proj_hbm, proj_ref.at[me], peer)]
    for copy in twin + sides + beyond + projs:
        copy.start()

    prepare_bias(lat, pos_ref, class_ref, pos_scr, class_scr)

    @pl.loop(0, bands)
    def _(s):
        row = jnp.where(lat == 1, bands - 1 - s, s)
        lane = lax.broadcasted_iota(jnp.int32, (128, size), 0) % 64
        cells = jnp.concatenate([cell_ref[pl.ds(4 * row + i, 1)] for i in range(4)], axis=1)
        flags = (lane == cells).astype(F32).astype(BF)
        block = lax.dot_general(
            order, flags, (((1,), (1,)), ((), ())), preferred_element_type=F32
        ).astype(BF)
        for level in range(2):
            hot[s, level, 1 : patches + 1] = block.reshape(patches, 16, 128)

    def normal(rows):
        return layer_norm(rows.astype(F32)).astype(BF)

    def project(normed, i):
        return jnp.dot(normed, qkv_ref[i], preferred_element_type=F32).astype(BF)

    def project_level(level):
        inside = slice(1, patches + 1)
        normed = normal(x[level, 0:bands, inside].reshape(bands * size, width))
        for i, ref in enumerate((q_scr, k_scr, v_scr)):
            got = project(normed, i)
            if i == 0:
                got = got * jnp.asarray(0.125, BF)
            ref[0:bands, level, inside] = got.reshape(bands, patches, 16, inner)

    for load in loads[:3]:
        load.wait()
    project_level(me)
    twin[0].wait_recv()
    project_level(other)
    def attend_windows(windows, places, first, stride):
        @pl.loop(0, places)
        def _(i):
            w = first + i * stride

            def rows(ref, slots, lanes):
                parts = [ref[s, :, pl.ds(2 * w, 2), :, lanes].reshape(64, 128) for s in slots]
                return parts[0] if len(parts) == 1 else jnp.concatenate(parts, axis=0)

            for pair in range(inner // 128):
                lanes = slice(pair * 128, pair * 128 + 128)
                for q_slots, k_slots, q_part, k_part in windows:
                    mixed = attend_pair(
                        rows(q_scr, q_slots, lanes),
                        rows(k_scr, k_slots, lanes),
                        rows(v_scr, k_slots, lanes),
                        rows(hot, q_slots, slice(None)),
                        pos_scr[2 * pair, q_part, k_part],
                        pos_scr[2 * pair + 1, q_part, k_part],
                        class_scr[2 * pair, k_part],
                        class_scr[2 * pair + 1, k_part],
                    )
                    for at, slot in enumerate(q_slots):
                        block = mixed[at * 64 : at * 64 + 64].reshape(2, 2, 16, 128)
                        att[me, slot, :, pl.ds(2 * w, 2), :, lanes] = block

    def share(first, last):
        part = att.at[me, first:last, :, 1 : patches + 1]
        copy = remote(part, part, peer)
        copy.start()
        return copy

    attend_windows(WINDOWS[:2], patches // 2 - 1, 1, 1)
    for copy in sides:
        copy.wait_recv()

    half = bands * 16
    ends = [(level, place) for level in range(2) for place in (0, patches + 1)]
    rows = [x[level, 0:bands, place].reshape(half, width) for level, place in ends]
    normed = normal(jnp.concatenate(rows, axis=0))
    for i, ref in ((1, k_scr), (2, v_scr)):
        got = project(normed, i)
        for at, (level, place) in enumerate(ends):
            part = got[at * half : at * half + half]
            ref[0:bands, level, place] = part.reshape(bands, 16, inner)

    attend_windows(WINDOWS[:2], 2, 0, patches // 2)
    early = share(0, bands - 1)
    for copy in beyond:
        copy.wait_recv()

    normed = normal(x[:, bands].reshape(2 * (size + 32), width))
    for i, ref in ((1, k_scr), (2, v_scr)):
        ref[bands] = project(normed, i).reshape(2, patches + 2, 16, inner)

    attend_windows(WINDOWS[2:], patches // 2 + 1, 0, 1)
    late = share(bands - 1, bands)
    for load in loads[3:]:
        load.wait()
    projs[0].wait_recv()
    early.wait_recv()
    pieces = 2
    group = send.shape[1] // size
    hidden_units = up_ref.shape[1] // pieces

    def feed(level, at):
        slots = slice(group * at, group * at + group)
        wide = x[level, slots, 1 : patches + 1].reshape(group * size, width).astype(F32)
        for half in range(2):
            mixed = att[half, slots, level, 1 : patches + 1].reshape(group * size, inner)
            if half == 0:
                total = jnp.dot(mixed, proj_ref[half], preferred_element_type=F32)
            else:
                total += jnp.dot(mixed, proj_ref[half], preferred_element_type=F32)
        wide = (wide + total).astype(BF).astype(F32)
        normed = normal(wide)
        total = None
        for piece in range(pieces):
            units = slice(piece * hidden_units, (piece + 1) * hidden_units)
            lifted = jnp.dot(normed, up_ref[:, units], preferred_element_type=F32)
            active = (0.5 * lifted * (1.0 + lax.erf(lifted * (0.5**0.5)))).astype(BF)
            part = jnp.dot(active, down_ref[units], preferred_element_type=F32)
            total = part if total is None else total + part
        return wide, total

    steps = bands // group
    returns = [remote(send.at[at], recv.at[at], peer) for at in range(steps)]
    for at in range(steps):
        if at == steps - 1:
            late.wait_recv()
        _, total = feed(other, at)
        send[at] = total.astype(BF)
        returns[at].start()

    back = band_order(size // 4)
    for at in range(steps):
        wide, total = feed(me, at)
        keep[...] = wide + total
        returns[at].wait_recv()
        for part in range(group):
            s = at * group + part
            row = jnp.where(lat == 1, bands - 1 - s, s)
            here = slice(part * size, (part + 1) * size)
            done = (keep[here] + recv[at, here].astype(F32)).astype(BF)
            out_ref[row] = lax.dot_general(
                back, done, (((0,), (0,)), ((), ())), preferred_element_type=F32
            ).astype(BF)

    for copy in twin + sides + beyond + projs + [early, late] + returns:
        copy.wait_send()


def body(
    tokens, qkv_weight, proj_weight, up_weight, down_weight, pos_bias, class_bias, surface_class
):
    heads = pos_bias.shape[0]
    _, tall, broad, width = tokens.shape
    inner, units = qkv_weight.shape[-1], up_weight.shape[-1]
    bands, patches, size = tall // 4, broad // 4, 4 * broad
    group = 4
    copies = 1 + 4 + 6 + 1 + 2 + bands // group
    vmem = pl.BlockSpec(memory_space=pltpu.VMEM)
    anywhere = pl.BlockSpec(memory_space=pl.ANY)
    scratch = (
        ((2, bands + 1, patches + 2, 16, width), BF),
        ((bands, 2, patches + 2, 16, inner), BF),
        ((bands + 1, 2, patches + 2, 16, inner), BF),
        ((bands + 1, 2, patches + 2, 16, inner), BF),
        ((bands, 2, patches + 2, 16, 128), BF),
        ((heads, 128, 128), F32),
        ((heads, 128, 128), BF),
        ((2, bands, 2, patches + 2, 16, inner), BF),
        ((group * size, width), F32),
        ((bands // group, group * size, width), BF),
        ((bands // group, group * size, width), BF),
        (qkv_weight.shape, BF),
        ((2,) + proj_weight.shape, BF),
        (up_weight.shape, BF),
        (down_weight.shape, BF),
    )
    out = pl.pallas_call(
        layer_kernel,
        out_shape=jax.ShapeDtypeStruct((bands, size, width), BF),
        in_specs=[vmem] * 4 + [anywhere] * 4,
        out_specs=vmem,
        scratch_shapes=[pltpu.VMEM(shape, kind) for shape, kind in scratch]
        + [
            pltpu.SemaphoreType.DMA((6,)),
            pltpu.SemaphoreType.DMA((copies,)),
            pltpu.SemaphoreType.DMA((copies,)),
        ],
        compiler_params=pltpu.CompilerParams(
            collective_id=0, has_side_effects=True, vmem_limit_bytes=58 * 2**20
        ),
        cost_estimate=pl.CostEstimate(
            flops=17 * 10**9, bytes_accessed=16 * 2**20, transcendentals=4 * 10**6
        ),
        name="window_layer",
    )(
        tokens.reshape(bands, size, width),
        surface_class,
        pos_bias,
        class_bias,
        qkv_weight,
        proj_weight,
        up_weight,
        down_weight,
    )
    return out.reshape(1, tall, broad, width)


def solution(mesh):
    placed = (
        P("tp", "lat", "lon", None),
        P(None, None, "tp"),
        P("tp", None),
        P(None, "tp"),
        P("tp", None),
        P("tp", None, None),
        P(None, "tp", None),
        P("lat", "lon"),
    )
    return jax.shard_map(
        body, mesh=mesh, in_specs=placed, out_specs=P("tp", "lat", "lon", None), check_vma=False
    )
```
